256 devices in a mesh: chain: 16 (over y, x), group: 16 (over z, core).
Axes of the slice: x: 4, y: 4, z: 8, core: 2. Of those that a mesh axis runs over, the one named last changes fastest.
Arguments:
- train_emb: bfloat16 [4096, 1024], P(('chain', 'group')), may hold values from -6 to 6
- cand_emb: bfloat16 [16384, 1024], P('group'), may hold values from -6 to 6
- factor: float32 [4096, 4096], P('chain'), may hold values from -0.09375 to 0.09375
- diag_inverse: float32 [4096, 256], P('chain'), as said below
- targets: float32 [4096], P('chain'), may hold values from -0.09375 to 0.09375
Outputs:
- whitened: float32 [4096, 16384], P('chain', 'group')
- post_mean: float32 [16384], P('group')
The draws below stay inside these ranges and needn't reach their ends.
Inputs may be any that keep to these rules, and one draw needn't show every extreme that they name: Each block of 256 rows of diag_inverse is lower triangular with a positive diagonal.
All inputs are finite; a program needn't handle non-finite values.
Results may differ from the reference program's by a relative error of at most 0.0003.
Values may be sent and summed in bfloat16 or wider, within the bound.
No kernel may reach another device: no remote copies, remote signals or barrier semaphores. Data moves between devices by JAX's collectives and lax.ppermute only.
A program may use at most 64 MiB of HBM per device.

```python
import math
import jax
import jax.numpy as jnp
from jax import lax

E = 1024
BS = 256
NTRAIN = 4096
CANDS = 16384


def draw_diag_inverse(key, part):
    first, second = jax.random.split(key)
    local = (jnp.arange(NTRAIN) % BS)[:, None]
    column = jnp.arange(BS)[None, :]
    offdiag = jax.random.normal(first, (NTRAIN, BS), jnp.float32)
    diagonal = jnp.exp(jax.random.uniform(second, (NTRAIN, 1), jnp.float32, jnp.log(0.5), jnp.log(1.5)))
    offdiag = offdiag * (0.8 / jnp.sqrt(jnp.float32(BS)))
    lower = jnp.where(column < local, offdiag, 0.0)
    return lower + jnp.where(column == local, diagonal, 0.0)


def block_scale(own_key, extent, pieces, least, high):
    gain, own = 1.0, jax.random.fold_in(own_key, 6)
    for position, parts in pieces:
        draws = jnp.exp(jax.random.uniform(jax.random.fold_in(own, position), (parts,), jnp.float32, least / len(pieces), high / len(pieces)))
        gain = gain * jnp.repeat(draws, extent[position] // parts).reshape([-1 if axis == position else 1 for axis in range(len(extent))])
    return gain


def bell_draw(stream_key, dims, spread, bound, pieces=(), kind=jnp.bfloat16):
    result = spread * jax.random.normal(stream_key, dims, jnp.float32)
    if pieces:
        result = result * block_scale(stream_key, dims, pieces, -0.22, 0.18)
    return jnp.clip(result, -bound, bound).astype(kind)


def setup_inputs(seed: int = 0) -> dict:
    keys = jax.random.split(jax.random.key(seed), 6)
    return {
        "train_emb": bell_draw(keys[0], (NTRAIN, E), 1.0, 6.0, ((0, 256),)),
        "cand_emb": bell_draw(keys[1], (CANDS, E), 1.0, 6.0, ((0, 16),)),
        "factor": bell_draw(keys[2], (NTRAIN, NTRAIN), NTRAIN ** -0.5, 0.09375, ((0, 16),), jnp.float32),
        "diag_inverse": draw_diag_inverse(jax.random.fold_in(keys[5], 71), 0),
        "targets": bell_draw(keys[4], (NTRAIN,), NTRAIN ** -0.5, 0.09375, ((0, 16),), jnp.float32),
    }


EPS = 1e-06

def reference(train_emb, cand_emb, factor, diag_inverse, targets):
    beta = 0.5 * math.sqrt(E)
    train_f = train_emb.astype(jnp.float32)
    cand_f = cand_emb.astype(jnp.float32)
    train_scale = lax.rsqrt(lax.optimization_barrier(jnp.sum(train_f * train_f, axis=1)) + EPS)
    cand_scale = lax.rsqrt(lax.optimization_barrier(jnp.sum(cand_f * cand_f, axis=1)) + EPS)
    cross = jnp.dot(train_emb, cand_emb.T, preferred_element_type=jnp.float32)
    panel = jnp.exp(beta * cross * train_scale[:, None] * cand_scale[None, :])
    blocks = []
    nblocks = NTRAIN // BS
    for index in range(nblocks):
        rows = panel[index * BS:(index + 1) * BS]
        if index > 0:
            earlier = jnp.concatenate(blocks, axis=0)
            rows = rows - jnp.dot(factor[index * BS:(index + 1) * BS, :index * BS], earlier, precision=lax.Precision.HIGHEST, preferred_element_type=jnp.float32)
        solved = jnp.dot(diag_inverse[index * BS:(index + 1) * BS], rows, precision=lax.Precision.HIGHEST, preferred_element_type=jnp.float32)
        blocks.append(solved)
    whitened = jnp.concatenate(blocks, axis=0)
    post_mean = lax.optimization_barrier(jnp.sum(whitened * targets[:, None], axis=0))
    return (whitened, post_mean)
```

```python
import functools
import math

import jax
import jax.numpy as jnp
from jax import lax
from jax.experimental import pallas as pl
from jax.experimental.pallas import tpu as pltpu
from jax.sharding import PartitionSpec as P

EPS = 1e-06
BF16 = jnp.bfloat16
F32 = jnp.float32
AXES = ("chain", "group")
SIDE = 4
ZS = 8
VMEM = pl.BlockSpec(memory_space=pltpu.VMEM)
SMEM = pl.BlockSpec(memory_space=pltpu.SMEM)
PARAMS = pltpu.CompilerParams(vmem_limit_bytes=56 * 1024 * 1024)


def moves(target):
    pairs = []
    for y in range(SIDE):
        for x in range(SIDE):
            for z in range(ZS):
                for c in range(2):
                    to = target(y, x, z, c)
                    if to is not None:
                        ty, tx, tz, tc = to
                        source = ((y * SIDE + x) * ZS + z) * 2 + c
                        dest = ((ty * SIDE + tx) * ZS + tz) * 2 + tc
                        pairs.append((source, dest))
    return pairs


def send(value, target):
    return lax.ppermute(value, AXES, moves(target))


def swap_core(value):
    return send(value, lambda y, x, z, c: (y, x, z, 1 - c))


def split(a):
    hi = a.astype(BF16)
    return hi, (a - hi.astype(F32)).astype(BF16)


def mul(a, b, dims):
    return lax.dot_general(a, b, (dims, ((), ())), preferred_element_type=F32)


NT = ((1,), (1,))
NN = ((1,), (0,))


def mul3(a, b, dims):
    (ah, al), (bh, bl) = a, b
    return mul(ah, bh, dims) + (mul(ah, bl, dims) + mul(al, bh, dims))


def nt(a, b):
    return mul3(split(a), split(b), NT)


def prepare_kernel(index_ref, f_ref, hi_ref, lo_ref):
    hi, lo = split(f_ref[...])
    hi_ref[0] = hi
    lo_ref[0] = lo


def prepare(factor, index, bs):
    count = index.shape[0]
    spec = pl.BlockSpec((1, bs, bs), lambda i, idx: (i, 0, 0))
    shape = jax.ShapeDtypeStruct((count, bs, bs), BF16)
    return pl.pallas_call(
        prepare_kernel,
        grid_spec=pltpu.PrefetchScalarGridSpec(
            num_scalar_prefetch=1,
            grid=(count,),
            in_specs=[pl.BlockSpec((bs, bs), lambda i, idx: (0, idx[i]))],
            out_specs=[spec, spec],
        ),
        out_shape=[shape, shape],
        compiler_params=PARAMS,
    )(index, factor)


def diagonal_kernel(place, d_ref, p1, p2, p3, r1, r2, r3, s1, s2, s3, out_ref):
    bs = d_ref.shape[0]
    x, c = place[0], place[1]
    first = c == 0
    dc, db, da = (jnp.where(first, r[...], s[...]) for r, s in ((r1, s1), (r2, s2), (r3, s3)))
    fcb, fba, fca = (jnp.where(first, s[...], r[...]) for r, s in ((r1, s1), (r2, s2), (r3, s3)))
    own = d_ref[...]
    dct, dbt, dat = dc.T, db.T, da.T
    sba = -nt(nt(dat, fba), db)
    ab = nt(jnp.concatenate([dbt, sba], 0), fcb)
    both = jnp.concatenate([ab[:bs], ab[bs:] + nt(dat, fca)], 0)
    cc = -nt(both, dc)
    scb, sca = cc[:bs], cc[bs:]
    t1 = nt(jnp.concatenate([dct, scb, sca], 0), p1[...])
    t2 = nt(jnp.concatenate([dbt, sba], 0), p2[...])
    t3 = nt(dat, p3[...])
    rows = jnp.concatenate([t1[:bs], t1[bs : 2 * bs] + t2[:bs], t1[2 * bs :] + t2[bs:] + t3], 0)
    res = -nt(rows, own)
    out_ref[...] = jnp.zeros_like(out_ref)
    out_ref[pl.ds(pl.multiple_of(x * bs, bs), bs), :] = own.T
    for k in (1, 2, 3):

        @pl.when(x >= k)
        def _():
            at = pl.multiple_of(jnp.maximum(x - k, 0) * bs, bs)
            out_ref[pl.ds(at, bs), :] = res[(k - 1) * bs : k * bs]


def diagonal(place, d, prev, near, far):
    bs = d.shape[0]
    return pl.pallas_call(
        diagonal_kernel,
        in_specs=[SMEM] + [VMEM] * 10,
        out_specs=VMEM,
        out_shape=jax.ShapeDtypeStruct((SIDE * bs, bs), F32),
        compiler_params=PARAMS,
    )(place, d, *prev, *near, *far)


def times_factor_kernel(count, init, *refs):
    xs, (hi, lo), rest = refs[:count], refs[count : count + 2], refs[count + 2 :]
    total = rest[0][...] if init else None
    for i in range(count):
        part = mul3(split(xs[i][...]), (hi[i], lo[i]), NT)
        total = part if total is None else total + part
    rest[-1][...] = total


def times_factor(xs, weights, first, init=None):
    n, (m, bs) = len(xs), xs[0].shape
    wspec = pl.BlockSpec((n, bs, bs), lambda i: (first, 0, 0))
    small = pl.BlockSpec((m, bs), lambda i: (0, 0))
    extra = [] if init is None else [init]
    return pl.pallas_call(
        functools.partial(times_factor_kernel, n, init is not None),
        grid=(1,),
        in_specs=[small] * n + [wspec, wspec] + [small] * len(extra),
        out_specs=small,
        out_shape=jax.ShapeDtypeStruct((m, bs), F32),
        compiler_params=PARAMS,
    )(*xs, *weights, *extra)


def times_inverse_kernel(below, place, *refs):
    ts, st = refs[:SIDE], refs[SIDE]
    out = refs[-1]
    bs = st.shape[1]
    x, c = place[0], place[1]
    total = None
    for k in range(SIDE):
        at = pl.multiple_of(jnp.maximum(x - k, 0) * bs, bs)
        part = mul3(split(ts[k][...]), split(st[pl.ds(at, bs), :]), NN)
        total = part if total is None else total + part
    if below:
        qs, ma, mb = refs[SIDE + 1 : 2 * SIDE + 1], refs[2 * SIDE + 1], refs[2 * SIDE + 2]
        full = refs[2 * SIDE + 4]
        interleave(full, ma, mb, c)
        for k in range(SIDE):
            at = pl.multiple_of(lax.rem(x - k + SIDE, SIDE) * bs, bs)
            total = total + mul3(split(qs[k][...]), split(full[pl.ds(at, bs), :]), NN)
        out = refs[2 * SIDE + 3]
    out[...] = -total


def interleave(full, ma, mb, c):
    m = ma.shape[1]
    for z in range(ZS):
        full[pl.ds(pl.multiple_of((2 * z + c) * m, m), m), :] = ma[z]
        full[pl.ds(pl.multiple_of((2 * z + 1 - c) * m, m), m), :] = mb[z]


def times_inverse(place, ts, st, below=None):
    m, bs = ts[0].shape
    args, scratch = [*ts, st], []
    if below is not None:
        qs, ma, mb = below
        args += [*qs, ma, mb]
        scratch = [pltpu.VMEM((SIDE * bs, bs), F32)]
    return pl.pallas_call(
        functools.partial(times_inverse_kernel, below is not None),
        in_specs=[SMEM] + [VMEM] * len(args),
        out_specs=VMEM,
        out_shape=jax.ShapeDtypeStruct((m, bs), F32),
        scratch_shapes=scratch,
        compiler_params=PARAMS,
    )(place, *args)


def panel_kernel(beta, train_ref, cand_ref, scale_ref, hi_ref, lo_ref):
    rows = train_ref[...]
    rows_f = rows.astype(F32)
    row_scale = lax.rsqrt(jnp.sum(rows_f * rows_f, axis=1, keepdims=True) + EPS)
    cross = mul(rows, cand_ref[...], NT)
    hi, lo = split(jnp.exp(beta * cross * row_scale * scale_ref[...]))
    hi_ref[...] = hi
    lo_ref[...] = lo


def make_panel(train, cand, cand_scale, rows):
    total, e = train.shape
    n = cand.shape[0]
    spec = pl.BlockSpec((rows, n), lambda i: (i, 0))
    shape = jax.ShapeDtypeStruct((total, n), BF16)
    return pl.pallas_call(
        functools.partial(panel_kernel, 0.5 * math.sqrt(e)),
        grid=(total // rows,),
        in_specs=[
            pl.BlockSpec((rows, e), lambda i: (i, 0)),
            pl.BlockSpec((n, e), lambda i: (0, 0)),
            pl.BlockSpec((1, n), lambda i: (0, 0)),
        ],
        out_specs=[spec, spec],
        out_shape=[shape, shape],
        compiler_params=PARAMS,
    )(train, cand, cand_scale)


def arrange_kernel(place, *refs):
    z = place[2]
    out = refs[-1]
    for k in range(ZS):
        out[lax.rem(z - k + ZS, ZS)] = refs[k][...]


def z_gather(place, own):
    parts = [own]
    for k in range(1, ZS):
        parts.append(send(own, lambda y, x, z, c: (y, x, (z + k) % ZS, c)))
    mine = pl.pallas_call(
        arrange_kernel,
        in_specs=[SMEM] + [VMEM] * ZS,
        out_specs=VMEM,
        out_shape=jax.ShapeDtypeStruct((ZS,) + own.shape, own.dtype),
        compiler_params=PARAMS,
    )(place, *parts)
    return mine, swap_core(mine)


def apply_kernel(sliced, last, which, place, *refs):
    if sliced:
        ma, mb, refs = refs[0], refs[1], refs[2:]
    else:
        st, refs = refs[0], refs[1:]
    if sliced:
        win, refs = refs[0], refs[1:]
    hi, lo, refs = refs[0], refs[1], refs[2:]
    if last:
        targets, refs = refs[0], refs[1:]
    out, refs = refs[0], refs[1:]
    if last:
        mean, refs = refs[0], refs[1:]
    mh, ml = refs[-2], refs[-1]
    bs = mh.shape[0]
    step = pl.program_id(0)

    @pl.when(step == 0)
    def _():
        if sliced:
            full = refs[0]
            interleave(full, ma, mb, place[1])
            wide = full[...].T
            out[...] = win[...]
        else:
            wide = st[...].T
            out[...] = jnp.zeros_like(out)
        h, l = split(wide)
        mh[...] = h
        ml[...] = l

    at = pl.ds(pl.multiple_of(step * bs, bs), bs)
    out[...] += mul3((mh[:, at], ml[:, at]), (hi[...], lo[...]), NN)
    if last:

        @pl.when(step == pl.num_programs(0) - 1)
        def _():
            mean[...] = jnp.sum(out[...] * targets[...], axis=0, keepdims=True)


def apply(which, place, inverse, panel, win=None, targets=None):
    hi, lo = panel
    n = hi.shape[1]
    sliced, last = win is not None, targets is not None
    bs = inverse[0].shape[-1]
    steps = SIDE
    fixed = lambda shape: pl.BlockSpec(shape, lambda i, w, p: (0,) * len(shape))
    pspec = pl.BlockSpec((bs, n), lambda i, w, p: (w[0] * SIDE + i, 0))
    args = list(inverse)
    specs = [fixed(a.shape) for a in args]
    if sliced:
        args.append(win)
        specs.append(fixed(win.shape))
    args += [hi, lo]
    specs += [pspec, pspec]
    if last:
        args.append(targets)
        specs.append(fixed(targets.shape))
    shapes = [jax.ShapeDtypeStruct((bs, n), F32)]
    if last:
        shapes.append(jax.ShapeDtypeStruct((1, n), F32))
    scratch = [pltpu.VMEM((bs, SIDE * bs), BF16)] * 2
    if sliced:
        scratch = [pltpu.VMEM((SIDE * bs, bs), F32)] + scratch
    return pl.pallas_call(
        functools.partial(apply_kernel, sliced, last),
        grid_spec=pltpu.PrefetchScalarGridSpec(
            num_scalar_prefetch=2,
            grid=(steps,),
            in_specs=specs,
            out_specs=[fixed(s.shape) for s in shapes],
            scratch_shapes=scratch,
        ),
        out_shape=shapes,
        compiler_params=PARAMS,
    )(which, place, *args)


def up_x(k, value):
    return send(value, lambda y, x, z, c: (y, x + k, z, c) if x + k < SIDE else None)


def spread_y(value, rows):
    return [
        send(value, lambda y, x, z, c: (rows[y], (x + k) % SIDE, z, c) if y in rows else None)
        for k in range(SIDE)
    ]


def shards(train_emb, cand_emb, factor, diag_inverse, targets):
    bs = diag_inverse.shape[1]
    n = cand_emb.shape[0]
    p = lax.axis_index("chain")
    group = lax.axis_index("group")
    y, x, z, c = p // SIDE, p % SIDE, group // 2, group % 2
    place = jnp.stack([x, c, z, y]).astype(jnp.int32)

    def block(back):
        return lax.dynamic_slice(factor, (0, jnp.maximum(p - back, 0) * bs), (bs, bs))

    prev = [block(k) for k in (1, 2, 3)]
    even = c == 0
    pay = jnp.where(even, diag_inverse, prev[0])
    pay3 = jnp.where(even, diag_inverse, prev[1])

    def to1(y, x, z, c):
        return (y, x + 1, z, c) if x < 3 and (c == 0 or x >= 1) else None

    def to2(y, x, z, c):
        return (y, x + 2, z, c) if x < 2 and (c == 0 or x == 1) else None

    def to3(y, x, z, c):
        return (y, 3, z, c) if (c == 0 and x == 0) or (c == 1 and x == 2) else None

    near = [send(pay, to1), send(pay, to2), send(pay3, to3)]
    far = [swap_core(v) for v in near]
    index = jnp.stack(
        [jnp.maximum(y - dy, 0) * SIDE + lax.rem(x - dx + SIDE, SIDE) for dy in (1, 2, 3) for dx in range(SIDE)]
    ).astype(jnp.int32)
    weights = prepare(factor, index, bs)
    st = diagonal(place, diag_inverse, prev, near, far)

    m = SIDE * bs // (2 * ZS)
    sl = lax.dynamic_slice(st, (group * m, 0), (m, bs))
    s1 = spread_y(sl, {0: 1, 1: 2, 2: 3})
    t1 = times_factor(s1, weights, 0)
    t1_low = [t1] + [up_x(k, t1) for k in (1, 2, 3)]
    m1 = times_inverse(place, t1_low, st)

    s2 = spread_y(sl, {0: 2, 1: 3})
    s3 = spread_y(sl, {0: 3})
    t2 = times_factor(s2, weights, 1)
    t3 = times_factor(s3, weights, 2)

    m10_2 = spread_y(m1, {1: 2})
    m10_3 = spread_y(m1, {1: 3})
    m1_full = z_gather(place, m1)

    q1 = spread_y(t1, {2: 3})
    t31_low = [t2] + [up_x(k, t2) for k in (1, 2, 3)]
    m31 = times_inverse(place, t31_low, st, (q1, *m1_full))
    m31 = jnp.where(y == 3, m31, jnp.zeros_like(m31))
    ma_full = z_gather(place, m31)

    t20 = times_factor(m10_2, weights, 0, t2)
    t30 = times_factor(m10_3, weights, 1, t3)
    t0 = jnp.where(y == 3, t30, t20)
    q0 = spread_y(t0, {2: 3})
    t0_low = [t0] + [up_x(k, t0) for k in (1, 2, 3)]
    mb = times_inverse(place, t0_low, st, (q0, *m1_full))
    mb = jnp.where(y >= 2, mb, jnp.zeros_like(mb))
    mb_full = z_gather(place, mb)

    cand_f = cand_emb.astype(F32)
    cand_scale = lax.rsqrt(jnp.sum(cand_f * cand_f, axis=1) + EPS).reshape(1, n)
    train = lax.all_gather(train_emb, AXES, axis=0, tiled=True)
    panel = make_panel(train, cand_emb, cand_scale, 2 * bs)

    at = lambda v: jnp.full((1,), v, jnp.int32)
    (w,) = apply(at(y), place, (st,), panel)
    (w,) = apply(at(jnp.maximum(y - 1, 0)), place, m1_full, panel, w)
    (w,) = apply(at(1), place, ma_full, panel, w)
    w, mean = apply(at(0), place, mb_full, panel, w, targets.reshape(bs, 1))
    for axis in ("x", "y"):
        parts = [mean]
        for k in (1, 2, 3):
            if axis == "x":
                parts.append(send(mean, lambda y, x, z, c: (y, (x + k) % SIDE, z, c)))
            else:
                parts.append(send(mean, lambda y, x, z, c: ((y + k) % SIDE, x, z, c)))
        mean = (parts[0] + parts[1]) + (parts[2] + parts[3])
    return w, mean.reshape(n)


def solution(mesh):
    in_specs = (
        P(("chain", "group"), None),
        P("group", None),
        P("chain", None),
        P("chain", None),
        P("chain"),
    )
    out_specs = (P("chain", "group"), P("group"))
    return jax.shard_map(shards, mesh=mesh, in_specs=in_specs, out_specs=out_specs, check_vma=False)
```

```python
import functools
import math

import jax
import jax.numpy as jnp
from jax import lax
from jax.experimental import pallas as pl
from jax.experimental.pallas import tpu as pltpu
from jax.sharding import PartitionSpec as P

EPS = 1e-06
BF16 = jnp.bfloat16
F32 = jnp.float32
AXES = ("chain", "group")
SIDE = 4
ZS = 8
VMEM = pl.BlockSpec(memory_space=pltpu.VMEM)
SMEM = pl.BlockSpec(memory_space=pltpu.SMEM)
PARAMS = pltpu.CompilerParams(vmem_limit_bytes=56 * 1024 * 1024)


def moves(target):
    pairs = []
    for y in range(SIDE):
        for x in range(SIDE):
            for z in range(ZS):
                for c in range(2):
                    to = target(y, x, z, c)
                    if to is not None:
                        ty, tx, tz, tc = to
                        source = ((y * SIDE + x) * ZS + z) * 2 + c
                        dest = ((ty * SIDE + tx) * ZS + tz) * 2 + tc
                        pairs.append((source, dest))
    return pairs


def send(value, target):
    return lax.ppermute(value, AXES, moves(target))


def swap_core(value):
    return send(value, lambda y, x, z, c: (y, x, z, 1 - c))


def x_ring(value):
    return [value] + [send(value, lambda y, x, z, c: (y, (x + k) % SIDE, z, c)) for k in (1, 2, 3)]


def y_ring(value):
    return [value] + [send(value, lambda y, x, z, c: ((y + k) % SIDE, x, z, c)) for k in (1, 2, 3)]


def hop(value, dy, dx=0):
    return send(value, lambda y, x, z, c: (y + dy, (x + dx) % SIDE, z, c) if y + dy < SIDE else None)


def split(a):
    hi = a.astype(BF16)
    return hi, (a - hi.astype(F32)).astype(BF16)


def mul(a, b, dims):
    return lax.dot_general(a, b, (dims, ((), ())), preferred_element_type=F32)


NT = ((1,), (1,))
NN = ((1,), (0,))


def mul3(a, b, dims):
    (ah, al), (bh, bl) = a, b
    return mul(ah, bh, dims) + (mul(ah, bl, dims) + mul(al, bh, dims))


def nt(a, b):
    return mul3(split(a), split(b), NT)


def spot(k, x, bs):
    return pl.ds(pl.multiple_of(lax.rem(x - k + SIDE, SIDE) * bs, bs), bs)


def diagonal_kernel(place, d_ref, f_ref, near, far, out_ref, d, f):
    bs = d_ref.shape[0]
    x, c = place[0], place[1]
    own = (d_ref[...], f_ref[:, :bs], f_ref[:, bs : 2 * bs], f_ref[:, 2 * bs : 3 * bs])
    d[x] = own[0]
    for j in range(3):
        f[x, j] = own[1 + j]
    for k in (1, 2, 3):
        at = lax.rem(x - k + SIDE, SIDE)

        @pl.when(c == 0)
        def _():
            d[at], f[at, 0] = near[k - 1, :bs], near[k - 1, bs:]
            f[at, 1], f[at, 2] = far[k - 1, :bs], far[k - 1, bs:]

        @pl.when(c == 1)
        def _():
            d[at], f[at, 0] = far[k - 1, :bs], far[k - 1, bs:]
            f[at, 1], f[at, 2] = near[k - 1, :bs], near[k - 1, bs:]

    out_ref[...] = jnp.zeros_like(out_ref)
    columns = []
    for i in range(SIDE):
        above = []
        for k in range(i):
            part = nt(columns[k], f[i, k])
            for j in range(k + 1):
                piece = part[j * bs : (j + 1) * bs]
                if j < len(above):
                    above[j] = above[j] + piece
                else:
                    above.append(piece)
        column = d[i].T
        if above:
            column = jnp.concatenate([-nt(jnp.concatenate(above, 0), d[i]), column], 0)
        columns.append(column)
        out_ref[: (i + 1) * bs, i * bs : (i + 1) * bs] = column


def diagonal(place, d, f, near, far):
    bs = d.shape[0]
    return pl.pallas_call(
        diagonal_kernel,
        in_specs=[SMEM] + [VMEM] * 4,
        out_specs=VMEM,
        out_shape=jax.ShapeDtypeStruct((SIDE * bs, SIDE * bs), F32),
        scratch_shapes=[pltpu.VMEM((SIDE, bs, bs), F32), pltpu.VMEM((SIDE, 3, bs, bs), F32)],
        compiler_params=PARAMS,
    )(place, d, f, near, far)


def first_factor_kernel(place, s_ref, f_ref, out_ref):
    out_ref[...] = nt(s_ref[...], f_ref[...])


def first_factor(place, s, factor):
    m, size = s.shape
    bs = factor.shape[0]
    return pl.pallas_call(
        first_factor_kernel,
        grid_spec=pltpu.PrefetchScalarGridSpec(
            num_scalar_prefetch=1,
            grid=(1,),
            in_specs=[
                pl.BlockSpec((m, size), lambda i, p: (0, 0)),
                pl.BlockSpec((bs, size), lambda i, p: (0, jnp.maximum(p[3] - 1, 0))),
            ],
            out_specs=pl.BlockSpec((m, bs), lambda i, p: (0, 0)),
        ),
        out_shape=jax.ShapeDtypeStruct((m, bs), F32),
        compiler_params=PARAMS,
    )(place, s, factor)


def first_inverse_kernel(place, t0, t1, t2, t3, st, out_ref, own_ref, t):
    x = place[0]
    bs = t0.shape[1]
    for k, ref in enumerate((t0, t1, t2, t3)):
        t[:, spot(k, x, bs)] = ref[...]
    out_ref[...] = -mul3(split(t[...]), split(st[...]), NN)
    own_ref[...] = out_ref[:, spot(0, x, bs)]


def first_inverse(place, ts, st):
    m, bs = ts[0].shape
    size = SIDE * bs
    return pl.pallas_call(
        first_inverse_kernel,
        in_specs=[SMEM] + [VMEM] * (SIDE + 1),
        out_specs=[VMEM, VMEM],
        out_shape=[jax.ShapeDtypeStruct((m, size), F32), jax.ShapeDtypeStruct((m, bs), F32)],
        scratch_shapes=[pltpu.VMEM((m, size), F32)],
        compiler_params=PARAMS,
    )(place, *ts, st)


def second_factor_kernel(place, s2, s3, m1, m2, t1, f_ref, out_ref):
    m, size = s2.shape
    y = place[3]
    low = y == 2
    zero = nt(jnp.where(low, s2[...], s3[...]), f_ref[:, :size])
    both = jnp.concatenate([jnp.where(low, m1[...], m2[...]), s2[...]], 0)
    both = nt(both, f_ref[:, size:])
    out_ref[:m] = jnp.where(y >= 2, zero + both[:m], 0.0)
    out_ref[m:] = jnp.where(low, t1[...], jnp.where(y == 3, both[m:], 0.0))


def second_factor(place, s2, s3, m1, m2, t1, factor):
    m, bs = t1.shape
    args = (s2, s3, m1, m2, t1)
    return pl.pallas_call(
        second_factor_kernel,
        grid=(1,),
        in_specs=[SMEM]
        + [pl.BlockSpec(a.shape, lambda i: (0, 0)) for a in args]
        + [pl.BlockSpec((bs, 2 * SIDE * bs), lambda i: (0, 0))],
        out_specs=pl.BlockSpec((2 * m, bs), lambda i: (0, 0)),
        out_shape=jax.ShapeDtypeStruct((2 * m, bs), F32),
        compiler_params=PARAMS,
    )(place, *args, factor)


def interleave(full, mine, other, c):
    m = full.shape[0] // (2 * ZS)
    for z in range(ZS):
        full[pl.ds(pl.multiple_of((2 * z + c) * m, m), m), :] = mine[z]
        full[pl.ds(pl.multiple_of((2 * z + 1 - c) * m, m), m), :] = other[z]


def second_inverse_kernel(place, *refs):
    ts, qs, (st, ma, mb, out_ref, t, q, full) = refs[:SIDE], refs[SIDE : 2 * SIDE], refs[2 * SIDE :]
    x, c, y = place[0], place[1], place[3]
    m, bs = ts[0].shape
    for k in range(SIDE):
        t[:, spot(k, x, bs)] = ts[k][...]
        q[:, spot(k, x, bs)] = qs[k][...]
    interleave(full, ma, mb, c)
    total = mul3(split(t[...]), split(st[...]), NN)
    below = mul3(split(q[...]), split(full[...]), NN)
    total = total + jnp.where(y == 3, below, 0.0)
    half = m // 2
    out_ref[:half] = jnp.where(y >= 2, -total[:half], 0.0)
    out_ref[half:] = jnp.where(y == 3, -total[half:], 0.0)


def second_inverse(place, ts, qs, st, ma, mb):
    m, bs = ts[0].shape
    size = SIDE * bs
    fixed = lambda a: pl.BlockSpec(a.shape, lambda i, p: (0,) * a.ndim)
    return pl.pallas_call(
        second_inverse_kernel,
        grid_spec=pltpu.PrefetchScalarGridSpec(
            num_scalar_prefetch=1,
            grid=(1,),
            in_specs=[fixed(a) for a in (*ts, *qs)]
            + [pl.BlockSpec((size, bs), lambda i, p: (0, p[0])), fixed(ma), fixed(mb)],
            out_specs=pl.BlockSpec((m, bs), lambda i, p: (0, 0)),
            scratch_shapes=[pltpu.VMEM((m, size), F32)] * 2 + [pltpu.VMEM((size, bs), F32)],
        ),
        out_shape=jax.ShapeDtypeStruct((m, bs), F32),
        compiler_params=PARAMS,
    )(place, *ts, *qs, st, ma, mb)


def panel_kernel(beta, train_ref, cand_ref, scale_ref, hi_ref, lo_ref):
    rows = train_ref[...]
    wide = rows.astype(F32)
    square = jnp.sum(wide * wide, axis=1, keepdims=True)
    row = jnp.broadcast_to(beta * lax.rsqrt(square + EPS), (rows.shape[0], 128)).T[:1]
    hi, lo = split(jnp.exp(mul(cand_ref[...], rows, NT) * row * scale_ref[...]))
    hi_ref[0] = hi
    lo_ref[0] = lo


def make_panel(train, cand, cand_scale, size):
    total, e = train.shape
    n = cand.shape[0]
    rows = size // 2
    spec = pl.BlockSpec((1, n, rows), lambda i: (i // 2, 0, i % 2))
    shape = jax.ShapeDtypeStruct((total // size, n, size), BF16)
    return pl.pallas_call(
        functools.partial(panel_kernel, 0.5 * math.sqrt(e)),
        grid=(total // rows,),
        in_specs=[
            pl.BlockSpec((rows, e), lambda i: (i, 0)),
            pl.BlockSpec((n, e), lambda i: (0, 0)),
            pl.BlockSpec((n, 1), lambda i: (0, 0)),
        ],
        out_specs=[spec, spec],
        out_shape=[shape, shape],
        cost_estimate=pl.CostEstimate(flops=4 * total * n * e, bytes_accessed=6 * total * n, transcendentals=total * n),
        compiler_params=PARAMS,
    )(train, cand, cand_scale)


def arrange_kernel(place, *refs):
    z = place[2]
    out = refs[-1]
    for k in range(ZS):
        out[lax.rem(z - k + ZS, ZS)] = refs[k][...]


def z_gather(place, own):
    parts = [own]
    for k in range(1, ZS):
        parts.append(send(own, lambda y, x, z, c: (y, x, (z + k) % ZS, c)))
    mine = pl.pallas_call(
        arrange_kernel,
        in_specs=[SMEM] + [VMEM] * ZS,
        out_specs=VMEM,
        out_shape=jax.ShapeDtypeStruct((ZS,) + own.shape, own.dtype),
        compiler_params=PARAMS,
    )(place, *parts)
    return mine, swap_core(mine)


def apply_kernel(last, sup, place, *refs):
    if last:
        m2, win, h0, l0, h1, l1, targets, out, mean, full, mh, ml = refs
    else:
        st, mine, other, h0, l0, h1, l1, out, full, mh, ml = refs
    size = full.shape[0]

    @pl.when(pl.program_id(0) == 0)
    def _():
        if last:
            m = size // (2 * ZS)
            for g in range(2 * ZS):
                full[g * m : (g + 1) * m] = m2[g, :m]
            mh[:size], ml[:size] = split(full[...])
            for g in range(2 * ZS):
                full[g * m : (g + 1) * m] = m2[g, m:]
        else:
            mh[:size], ml[:size] = split(st[...])
            interleave(full, mine, other, place[1])
        mh[size:], ml[size:] = split(full[...])

    w = mul3((h0[0], l0[0]), (mh[:size], ml[:size]), NN)
    w = w + mul3((h1[0], l1[0]), (mh[size:], ml[size:]), NN)
    if last:
        w = (w + win[...]).T
        out[...] = w
        mean[...] = jnp.sum(w * targets[...], axis=0, keepdims=True)
    else:
        out[...] = w


def apply(sup, place, arrays, panel, bs, targets=None):
    _, n, size = panel[0].shape
    last = targets is not None
    tile = n // 2
    fixed = lambda shape: pl.BlockSpec(shape, lambda i, s, p: (0,) * len(shape))
    args = [*arrays, *panel, *panel]
    specs = [fixed(a.shape) for a in arrays]
    across = pl.BlockSpec((tile, bs), lambda i, s, p: (i, 0))
    if last:
        specs[1] = across
    else:
        specs[0] = pl.BlockSpec((size, bs), lambda i, s, p: (0, p[0]))
    specs += [pl.BlockSpec((1, tile, size), lambda i, s, p: (s[0], i, 0))] * 2
    specs += [pl.BlockSpec((1, tile, size), lambda i, s, p: (s[1], i, 0))] * 2
    shapes, outs = [jax.ShapeDtypeStruct((n, bs), F32)], [across]
    if last:
        args.append(targets)
        specs.append(fixed(targets.shape))
        shapes = [jax.ShapeDtypeStruct((bs, n), F32), jax.ShapeDtypeStruct((1, n), F32)]
        outs = [pl.BlockSpec((bs, tile), lambda i, s, p: (0, i)), pl.BlockSpec((1, tile), lambda i, s, p: (0, i))]
    return pl.pallas_call(
        functools.partial(apply_kernel, last),
        grid_spec=pltpu.PrefetchScalarGridSpec(
            num_scalar_prefetch=2,
            grid=(n // tile,),
            in_specs=specs,
            out_specs=outs,
            scratch_shapes=[pltpu.VMEM((size, bs), F32)] + [pltpu.VMEM((2 * size, bs), BF16)] * 2,
        ),
        out_shape=shapes,
        cost_estimate=pl.CostEstimate(flops=24 * n * bs * size, bytes_accessed=8 * n * size, transcendentals=0),
        compiler_params=PARAMS,
    )(sup, place, *args)


def shards(train_emb, cand_emb, factor, diag_inverse, targets):
    bs = diag_inverse.shape[1]
    n = cand_emb.shape[0]
    size = SIDE * bs
    p = lax.axis_index("chain")
    group = lax.axis_index("group")
    y, x, z, c = p // SIDE, p % SIDE, group // 2, group % 2
    place = jnp.stack([x, c, z, y]).astype(jnp.int32)

    train = lax.all_gather(train_emb, AXES, axis=0, tiled=True)

    square = lax.dynamic_slice(factor, (0, y * size), (bs, size))
    pair0 = jnp.concatenate([diag_inverse, square[:, :bs]], 0)
    pair1 = jnp.concatenate([square[:, bs : 2 * bs], square[:, 2 * bs : 3 * bs]], 0)
    pair = jnp.where(c == 0, pair0, pair1)
    near = jnp.stack(
        [send(pair, lambda y, x, z, c: (y, (x + k) % SIDE, z, c) if c == 0 or x >= 2 else None) for k in (1, 2, 3)]
    )
    st = diagonal(place, diag_inverse, square, near, swap_core(near))

    m = size // (2 * ZS)
    sl = lax.dynamic_slice(st, (group * m, 0), (m, size))
    t1 = first_factor(place, hop(sl, 1), factor)
    m1, m1_own = first_inverse(place, x_ring(t1), st)
    t2 = second_factor(place, hop(sl, 2), hop(sl, 3), hop(m1, 1), hop(m1, 2), t1, factor)
    m1_full = z_gather(place, m1_own)
    m2 = second_inverse(place, x_ring(t2), [hop(t2, 1, k) for k in range(SIDE)], st, *m1_full)
    m2_full = lax.all_gather(m2, "group", axis=0)

    cand_f = cand_emb.astype(F32)
    cand_scale = lax.rsqrt(jnp.sum(cand_f * cand_f, axis=1, keepdims=True) + EPS)
    panel = make_panel(train, cand_emb, cand_scale, size)
    sup = jnp.stack([y, jnp.maximum(y - 1, 0)]).astype(jnp.int32)
    (w,) = apply(sup, place, (st, *m1_full), panel, bs)
    w, mean = apply(jnp.arange(2, dtype=jnp.int32), place, (m2_full, w), panel, bs, targets.reshape(bs, 1))
    for ring in (x_ring, y_ring):
        a, b, d, e = ring(mean)
        mean = (a + b) + (d + e)
    return w, mean.reshape(n)


def solution(mesh):
    in_specs = (
        P(("chain", "group"), None),
        P("group", None),
        P("chain", None),
        P("chain", None),
        P("chain"),
    )
    out_specs = (P("chain", "group"), P("group"))
    return jax.shard_map(shards, mesh=mesh, in_specs=in_specs, out_specs=out_specs, check_vma=False)
```

```python
import functools
import math

import jax
import jax.numpy as jnp
from jax import lax
from jax.experimental import pallas as pl
from jax.experimental.pallas import tpu as pltpu
from jax.sharding import Mesh
from jax.sharding import PartitionSpec as P

EPS = 1e-06
BF16 = jnp.bfloat16
F32 = jnp.float32
AXES = ("chain", "z", "c")
SIDE = 4
ZS = 8
CHAIN = SIDE * SIDE
VMEM = pl.BlockSpec(memory_space=pltpu.VMEM)
SMEM = pl.BlockSpec(memory_space=pltpu.SMEM)
PARAMS = pltpu.CompilerParams(vmem_limit_bytes=56 * 1024 * 1024)


def moves(target):
    pairs = []
    for y in range(SIDE):
        for x in range(SIDE):
            for z in range(ZS):
                for c in range(2):
                    to = target(y, x, z, c)
                    if to is not None:
                        ty, tx, tz, tc = to
                        source = ((y * SIDE + x) * ZS + z) * 2 + c
                        dest = ((ty * SIDE + tx) * ZS + tz) * 2 + tc
                        pairs.append((source, dest))
    return pairs


def send(value, target):
    return lax.ppermute(value, AXES, moves(target))


def swap_core(value):
    return send(value, lambda y, x, z, c: (y, x, z, 1 - c))


def x_ring(value):
    return [value] + [send(value, lambda y, x, z, c: (y, (x + k) % SIDE, z, c)) for k in (1, 2, 3)]


def hop(value, dy, dx=0):
    return send(value, lambda y, x, z, c: (y + dy, (x + dx) % SIDE, z, c) if y + dy < SIDE else None)


def split(a):
    hi = a.astype(BF16)
    return hi, (a - hi.astype(F32)).astype(BF16)


def mul(a, b, dims):
    return lax.dot_general(a, b, (dims, ((), ())), preferred_element_type=F32)


NT = ((1,), (1,))
NN = ((1,), (0,))


def mul3(a, b, dims):
    (ah, al), (bh, bl) = a, b
    return mul(ah, bh, dims) + (mul(ah, bl, dims) + mul(al, bh, dims))


def nt(a, b):
    return mul3(split(a), split(b), NT)


def spot(k, x, bs):
    return pl.ds(pl.multiple_of(lax.rem(x - k + SIDE, SIDE) * bs, bs), bs)


def diagonal_kernel(place, d_ref, f_ref, near, far, out_ref, d, f):
    bs = d_ref.shape[0]
    x, c = place[0], place[1]
    own = (d_ref[...], f_ref[:, :bs], f_ref[:, bs : 2 * bs], f_ref[:, 2 * bs : 3 * bs])
    d[x] = own[0]
    for j in range(3):
        f[x, j] = own[1 + j]
    for k in (1, 2, 3):
        at = lax.rem(x - k + SIDE, SIDE)

        @pl.when(c == 0)
        def _():
            d[at], f[at, 0] = near[k - 1, :bs], near[k - 1, bs:]
            f[at, 1], f[at, 2] = far[k - 1, :bs], far[k - 1, bs:]

        @pl.when(c == 1)
        def _():
            d[at], f[at, 0] = far[k - 1, :bs], far[k - 1, bs:]
            f[at, 1], f[at, 2] = near[k - 1, :bs], near[k - 1, bs:]

    out_ref[...] = jnp.zeros_like(out_ref)
    columns = []
    for i in range(SIDE):
        above = []
        for k in range(i):
            part = nt(columns[k], f[i, k])
            for j in range(k + 1):
                piece = part[j * bs : (j + 1) * bs]
                if j < len(above):
                    above[j] = above[j] + piece
                else:
                    above.append(piece)
        column = d[i].T
        if above:
            column = jnp.concatenate([-nt(jnp.concatenate(above, 0), d[i]), column], 0)
        columns.append(column)
        out_ref[: (i + 1) * bs, i * bs : (i + 1) * bs] = column


def diagonal(place, d, f, near, far):
    bs = d.shape[0]
    return pl.pallas_call(
        diagonal_kernel,
        in_specs=[SMEM] + [VMEM] * 4,
        out_specs=VMEM,
        out_shape=jax.ShapeDtypeStruct((SIDE * bs, SIDE * bs), F32),
        scratch_shapes=[pltpu.VMEM((SIDE, bs, bs), F32), pltpu.VMEM((SIDE, 3, bs, bs), F32)],
        compiler_params=PARAMS,
    )(place, d, f, near, far)


def first_factor_kernel(place, s_ref, f_ref, out_ref):
    out_ref[...] = nt(s_ref[...], f_ref[...])


def first_factor(place, s, factor):
    m, size = s.shape
    bs = factor.shape[0]
    return pl.pallas_call(
        first_factor_kernel,
        grid_spec=pltpu.PrefetchScalarGridSpec(
            num_scalar_prefetch=1,
            grid=(1,),
            in_specs=[
                pl.BlockSpec((m, size), lambda i, p: (0, 0)),
                pl.BlockSpec((bs, size), lambda i, p: (0, jnp.maximum(p[3] - 1, 0))),
            ],
            out_specs=pl.BlockSpec((m, bs), lambda i, p: (0, 0)),
        ),
        out_shape=jax.ShapeDtypeStruct((m, bs), F32),
        compiler_params=PARAMS,
    )(place, s, factor)


def first_inverse_kernel(place, t0, t1, t2, t3, st, out_ref, own_ref, t):
    x = place[0]
    bs = t0.shape[1]
    for k, ref in enumerate((t0, t1, t2, t3)):
        t[:, spot(k, x, bs)] = ref[...]
    th, tl = split(t[...])
    for i in range(SIDE):
        rows, columns = (i + 1) * bs, slice(i * bs, (i + 1) * bs)
        out_ref[:, columns] = -mul3((th[:, :rows], tl[:, :rows]), split(st[:rows, columns]), NN)
    own_ref[...] = out_ref[:, spot(0, x, bs)]


def first_inverse(place, ts, st):
    m, bs = ts[0].shape
    size = SIDE * bs
    return pl.pallas_call(
        first_inverse_kernel,
        in_specs=[SMEM] + [VMEM] * (SIDE + 1),
        out_specs=[VMEM, VMEM],
        out_shape=[jax.ShapeDtypeStruct((m, size), F32), jax.ShapeDtypeStruct((m, bs), F32)],
        scratch_shapes=[pltpu.VMEM((m, size), F32)],
        compiler_params=PARAMS,
    )(place, *ts, st)


def second_factor_kernel(place, s2, s3, m1, m2, t1, f_ref, out_ref):
    m, size = s2.shape
    y = place[3]
    low = y == 2
    zero = nt(jnp.where(low, s2[...], s3[...]), f_ref[:, :size])
    both = jnp.concatenate([jnp.where(low, m1[...], m2[...]), s2[...]], 0)
    both = nt(both, f_ref[:, size:])
    out_ref[:m] = jnp.where(y >= 2, zero + both[:m], 0.0)
    out_ref[m:] = jnp.where(low, t1[...], jnp.where(y == 3, both[m:], 0.0))


def second_factor(place, s2, s3, m1, m2, t1, factor):
    m, bs = t1.shape
    args = (s2, s3, m1, m2, t1)
    return pl.pallas_call(
        second_factor_kernel,
        grid=(1,),
        in_specs=[SMEM]
        + [pl.BlockSpec(a.shape, lambda i: (0, 0)) for a in args]
        + [pl.BlockSpec((bs, 2 * SIDE * bs), lambda i: (0, 0))],
        out_specs=pl.BlockSpec((2 * m, bs), lambda i: (0, 0)),
        out_shape=jax.ShapeDtypeStruct((2 * m, bs), F32),
        compiler_params=PARAMS,
    )(place, *args, factor)


def second_inverse_kernel(place, *refs):
    ts, qs, (st, below_ref, out_ref, t, q) = refs[:SIDE], refs[SIDE : 2 * SIDE], refs[2 * SIDE :]
    x, y = place[0], place[3]
    m, bs = ts[0].shape
    for k in range(SIDE):
        t[:, spot(k, x, bs)] = ts[k][...]
        q[:, spot(k, x, bs)] = qs[k][...]
    total = mul3(split(t[...]), split(st[...]), NN)
    below = mul3(split(q[...]), split(below_ref[...]), NN)
    total = total + jnp.where(y == 3, below, 0.0)
    half = m // 2
    out_ref[:half] = jnp.where(y >= 2, -total[:half], 0.0)
    out_ref[half:] = jnp.where(y == 3, -total[half:], 0.0)


def second_inverse(place, ts, qs, st, below):
    m, bs = ts[0].shape
    size = SIDE * bs
    fixed = lambda a: pl.BlockSpec(a.shape, lambda i, p: (0,) * a.ndim)
    return pl.pallas_call(
        second_inverse_kernel,
        grid_spec=pltpu.PrefetchScalarGridSpec(
            num_scalar_prefetch=1,
            grid=(1,),
            in_specs=[fixed(a) for a in (*ts, *qs)]
            + [pl.BlockSpec((size, bs), lambda i, p: (0, p[0])), fixed(below)],
            out_specs=pl.BlockSpec((m, bs), lambda i, p: (0, 0)),
            scratch_shapes=[pltpu.VMEM((m, size), F32)] * 2,
        ),
        out_shape=jax.ShapeDtypeStruct((m, bs), F32),
        compiler_params=PARAMS,
    )(place, *ts, *qs, st, below)


def panel_kernel(beta, train_ref, cand_ref, scale_ref, hi_ref, lo_ref):
    rows = train_ref[...]
    wide = rows.astype(F32)
    square = jnp.sum(wide * wide, axis=1, keepdims=True)
    row = jnp.broadcast_to(beta * lax.rsqrt(square + EPS), (rows.shape[0], 128)).T[:1]
    hi, lo = split(jnp.exp(mul(cand_ref[...], rows, NT) * row * scale_ref[...]))
    hi_ref[0] = hi
    lo_ref[0] = lo


def make_panel(train, cand, cand_scale, size):
    total, e = train.shape
    n = cand.shape[0]
    rows = size // 2
    spec = pl.BlockSpec((1, n, rows), lambda i: (i // 2, 0, i % 2))
    shape = jax.ShapeDtypeStruct((total // size, n, size), BF16)
    return pl.pallas_call(
        functools.partial(panel_kernel, 0.5 * math.sqrt(e)),
        grid=(total // rows,),
        in_specs=[
            pl.BlockSpec((rows, e), lambda i: (i, 0)),
            pl.BlockSpec((n, e), lambda i: (0, 0)),
            pl.BlockSpec((n, 1), lambda i: (0, 0)),
        ],
        out_specs=[spec, spec],
        out_shape=[shape, shape],
        cost_estimate=pl.CostEstimate(flops=4 * total * n * e, bytes_accessed=6 * total * n, transcendentals=total * n),
        compiler_params=PARAMS,
    )(train, cand, cand_scale)


def apply_kernel(last, sup, place, *refs):
    if last:
        m2, win, h0, l0, h1, l1, targets, out, mean, full, mh, ml = refs
    else:
        st, m1, h0, l0, h1, l1, out, full, mh, ml = refs
    size = full.shape[0]

    @pl.when(pl.program_id(0) == 0)
    def _():
        if last:
            m = size // (2 * ZS)
            for g in range(2 * ZS):
                full[g * m : (g + 1) * m] = m2[g, :m]
            mh[:size], ml[:size] = split(full[...])
            for g in range(2 * ZS):
                full[g * m : (g + 1) * m] = m2[g, m:]
        else:
            mh[:size], ml[:size] = split(st[...])
            full[...] = m1[...]
        mh[size:], ml[size:] = split(full[...])

    w = mul3((h0[0], l0[0]), (mh[:size], ml[:size]), NN)
    w = w + mul3((h1[0], l1[0]), (mh[size:], ml[size:]), NN)
    if last:
        w = (w + win[...]).T
        out[...] = w
        mean[...] = jnp.sum(w * targets[...], axis=0, keepdims=True)
    else:
        out[...] = w


def apply(sup, place, arrays, panel, bs, targets=None):
    _, n, size = panel[0].shape
    last = targets is not None
    tile = n // 2
    fixed = lambda shape: pl.BlockSpec(shape, lambda i, s, p: (0,) * len(shape))
    args = [*arrays, *panel, *panel]
    specs = [fixed(a.shape) for a in arrays]
    across = pl.BlockSpec((tile, bs), lambda i, s, p: (i, 0))
    if last:
        specs[1] = across
    else:
        specs[0] = pl.BlockSpec((size, bs), lambda i, s, p: (0, p[0]))
    specs += [pl.BlockSpec((1, tile, size), lambda i, s, p: (s[0], i, 0))] * 2
    specs += [pl.BlockSpec((1, tile, size), lambda i, s, p: (s[1], i, 0))] * 2
    shapes, outs = [jax.ShapeDtypeStruct((n, bs), F32)], [across]
    if last:
        args.append(targets)
        specs.append(fixed(targets.shape))
        shapes = [jax.ShapeDtypeStruct((bs, n), F32), jax.ShapeDtypeStruct((1, n), F32)]
        outs = [pl.BlockSpec((bs, tile), lambda i, s, p: (0, i)), pl.BlockSpec((1, tile), lambda i, s, p: (0, i))]
    return pl.pallas_call(
        functools.partial(apply_kernel, last),
        grid_spec=pltpu.PrefetchScalarGridSpec(
            num_scalar_prefetch=2,
            grid=(n // tile,),
            in_specs=specs,
            out_specs=outs,
            scratch_shapes=[pltpu.VMEM((size, bs), F32)] + [pltpu.VMEM((2 * size, bs), BF16)] * 2,
        ),
        out_shape=shapes,
        cost_estimate=pl.CostEstimate(flops=24 * n * bs * size, bytes_accessed=8 * n * size, transcendentals=0),
        compiler_params=PARAMS,
    )(sup, place, *args)


def z_gather(z, c, own):
    m, bs = own.shape
    parts = [own] + [send(own, lambda y, x, z, c: (y, x, (z - k) % ZS, c)) for k in range(1, ZS)]
    mine = jnp.stack(parts)
    other = swap_core(mine)
    even = c == 0
    both = jnp.stack([jnp.where(even, mine, other), jnp.where(even, other, mine)], 1)
    return jnp.roll(both, z, axis=0).reshape(2 * ZS * m, bs)


def shards(train_emb, cand_emb, factor, diag_inverse, targets):
    bs = diag_inverse.shape[1]
    n = cand_emb.shape[0]
    size = SIDE * bs
    p, z, c = (lax.axis_index(axis) for axis in AXES)
    y, x, group = p // SIDE, p % SIDE, 2 * z + c
    place = jnp.stack([x, c, z, y]).astype(jnp.int32)

    train = lax.all_gather(train_emb, AXES, axis=0, tiled=True)

    square = lax.dynamic_slice(factor, (0, y * size), (bs, size))
    pair0 = jnp.concatenate([diag_inverse, square[:, :bs]], 0)
    pair1 = jnp.concatenate([square[:, bs : 2 * bs], square[:, 2 * bs : 3 * bs]], 0)
    pair = jnp.where(c == 0, pair0, pair1)
    near = jnp.stack(
        [send(pair, lambda y, x, z, c: (y, (x + k) % SIDE, z, c) if c == 0 or x >= 2 else None) for k in (1, 2, 3)]
    )
    st = diagonal(place, diag_inverse, square, near, swap_core(near))

    m = size // (2 * ZS)
    sl = lax.dynamic_slice(st, (group * m, 0), (m, size))
    t1 = first_factor(place, hop(sl, 1), factor)
    t1, s2, s3 = lax.optimization_barrier((t1, hop(sl, 2), hop(sl, 3)))
    m1, m1_own = first_inverse(place, x_ring(t1), st)
    t2 = second_factor(place, s2, s3, hop(m1, 1), hop(m1, 2), t1, factor)
    m1_full = z_gather(z, c, m1_own)
    m2 = second_inverse(place, x_ring(t2), [hop(t2, 1, k) for k in range(SIDE)], st, m1_full)
    m2_full = lax.all_gather(m2, ("z", "c"), axis=0)

    train, _ = lax.optimization_barrier((train, m2))
    cand_f = cand_emb.astype(F32)
    cand_scale = lax.rsqrt(jnp.sum(cand_f * cand_f, axis=1, keepdims=True) + EPS)
    panel = make_panel(train, cand_emb, cand_scale, size)
    sup = jnp.stack([y, jnp.maximum(y - 1, 0)]).astype(jnp.int32)
    (w,) = apply(sup, place, (st, m1_full), panel, bs)
    w, mean = apply(jnp.arange(2, dtype=jnp.int32), place, (m2_full, w), panel, bs, targets.reshape(bs, 1))
    parts = lax.all_to_all(jnp.broadcast_to(mean, (CHAIN, n)), "chain", 0, 0, tiled=True)
    return w, jnp.sum(parts, axis=0)


def solution(mesh):
    fine = Mesh(mesh.devices.reshape(CHAIN, ZS, 2), AXES)
    group = ("z", "c")
    in_specs = (
        P(AXES, None),
        P(group, None),
        P("chain", None),
        P("chain", None),
        P("chain"),
    )
    out_specs = (P("chain", group), P(group))
    return jax.shard_map(shards, mesh=fine, in_specs=in_specs, out_specs=out_specs, check_vma=False)
```

```python
import functools
import math

import jax
import jax.numpy as jnp
from jax import lax
from jax.experimental import pallas as pl
from jax.experimental.pallas import tpu as pltpu
from jax.sharding import Mesh
from jax.sharding import PartitionSpec as P

EPS = 1e-06
BF16 = jnp.bfloat16
F32 = jnp.float32
AXES = ("chain", "z", "c")
SIDE = 4
ZS = 8
CHAIN = SIDE * SIDE
VMEM = pl.BlockSpec(memory_space=pltpu.VMEM)
SMEM = pl.BlockSpec(memory_space=pltpu.SMEM)
PARAMS = pltpu.CompilerParams(vmem_limit_bytes=56 * 1024 * 1024)


def moves(target):
    pairs = []
    for y in range(SIDE):
        for x in range(SIDE):
            for z in range(ZS):
                for c in range(2):
                    to = target(y, x, z, c)
                    if to is not None:
                        ty, tx, tz, tc = to
                        source = ((y * SIDE + x) * ZS + z) * 2 + c
                        dest = ((ty * SIDE + tx) * ZS + tz) * 2 + tc
                        pairs.append((source, dest))
    return pairs


def send(value, target):
    return lax.ppermute(value, AXES, moves(target))


def swap_core(value):
    return send(value, lambda y, x, z, c: (y, x, z, 1 - c))


def x_ring(value):
    return [value] + [send(value, lambda y, x, z, c: (y, (x + k) % SIDE, z, c)) for k in (1, 2, 3)]


def hop(value, dy, dx=0):
    return send(value, lambda y, x, z, c: (y + dy, (x + dx) % SIDE, z, c) if y + dy < SIDE else None)


def split(a):
    hi = a.astype(BF16)
    return hi, (a - hi.astype(F32)).astype(BF16)


def mul(a, b, dims):
    return lax.dot_general(a, b, (dims, ((), ())), preferred_element_type=F32)


NT = ((1,), (1,))
NN = ((1,), (0,))


def mul3(a, b, dims):
    (ah, al), (bh, bl) = a, b
    return mul(ah, bh, dims) + (mul(ah, bl, dims) + mul(al, bh, dims))


def nt(a, b):
    return mul3(split(a), split(b), NT)


def spot(k, x, bs):
    return pl.ds(pl.multiple_of(lax.rem(x - k + SIDE, SIDE) * bs, bs), bs)


def diagonal_kernel(place, d_ref, f_ref, near, far, out_ref, d, f):
    bs = d_ref.shape[0]
    x, c = place[0], place[1]
    own = (d_ref[...], f_ref[:, :bs], f_ref[:, bs : 2 * bs], f_ref[:, 2 * bs : 3 * bs])
    d[x] = own[0]
    for j in range(3):
        f[x, j] = own[1 + j]
    for k in (1, 2, 3):
        at = lax.rem(x - k + SIDE, SIDE)

        @pl.when(c == 0)
        def _():
            d[at], f[at, 0] = near[k - 1, :bs], near[k - 1, bs:]
            f[at, 1], f[at, 2] = far[k - 1, :bs], far[k - 1, bs:]

        @pl.when(c == 1)
        def _():
            d[at], f[at, 0] = far[k - 1, :bs], far[k - 1, bs:]
            f[at, 1], f[at, 2] = near[k - 1, :bs], near[k - 1, bs:]

    out_ref[...] = jnp.zeros_like(out_ref)
    columns = []
    for i in range(SIDE):
        above = []
        for k in range(i):
            part = nt(columns[k], f[i, k])
            for j in range(k + 1):
                piece = part[j * bs : (j + 1) * bs]
                if j < len(above):
                    above[j] = above[j] + piece
                else:
                    above.append(piece)
        column = d[i].T
        if above:
            column = jnp.concatenate([-nt(jnp.concatenate(above, 0), d[i]), column], 0)
        columns.append(column)
        out_ref[: (i + 1) * bs, i * bs : (i + 1) * bs] = column


def diagonal(place, d, f, near, far):
    bs = d.shape[0]
    return pl.pallas_call(
        diagonal_kernel,
        in_specs=[SMEM] + [VMEM] * 4,
        out_specs=VMEM,
        out_shape=jax.ShapeDtypeStruct((SIDE * bs, SIDE * bs), F32),
        scratch_shapes=[pltpu.VMEM((SIDE, bs, bs), F32), pltpu.VMEM((SIDE, 3, bs, bs), F32)],
        compiler_params=PARAMS,
    )(place, d, f, near, far)


def first_factor_kernel(place, s_ref, f_ref, out_ref):
    out_ref[...] = nt(s_ref[...], f_ref[...])


def first_factor(place, s, factor):
    m, size = s.shape
    bs = factor.shape[0]
    return pl.pallas_call(
        first_factor_kernel,
        grid_spec=pltpu.PrefetchScalarGridSpec(
            num_scalar_prefetch=1,
            grid=(1,),
            in_specs=[
                pl.BlockSpec((m, size), lambda i, p: (0, 0)),
                pl.BlockSpec((bs, size), lambda i, p: (0, jnp.maximum(p[3] - 1, 0))),
            ],
            out_specs=pl.BlockSpec((m, bs), lambda i, p: (0, 0)),
        ),
        out_shape=jax.ShapeDtypeStruct((m, bs), F32),
        compiler_params=PARAMS,
    )(place, s, factor)


def first_inverse_kernel(place, t0, t1, t2, t3, st, out_ref, own_ref, t):
    x = place[0]
    bs = t0.shape[1]
    for k, ref in enumerate((t0, t1, t2, t3)):
        t[:, spot(k, x, bs)] = ref[...]
    th, tl = split(t[...])
    for i in range(SIDE):
        rows, columns = (i + 1) * bs, slice(i * bs, (i + 1) * bs)
        out_ref[:, columns] = -mul3((th[:, :rows], tl[:, :rows]), split(st[:rows, columns]), NN)
    own_ref[...] = out_ref[:, spot(0, x, bs)]


def first_inverse(place, ts, st):
    m, bs = ts[0].shape
    size = SIDE * bs
    return pl.pallas_call(
        first_inverse_kernel,
        in_specs=[SMEM] + [VMEM] * (SIDE + 1),
        out_specs=[VMEM, VMEM],
        out_shape=[jax.ShapeDtypeStruct((m, size), F32), jax.ShapeDtypeStruct((m, bs), F32)],
        scratch_shapes=[pltpu.VMEM((m, size), F32)],
        compiler_params=PARAMS,
    )(place, *ts, st)


def second_factor_kernel(place, s2, s3, m1, m2, t1, f_ref, out_ref):
    m, size = s2.shape
    y = place[3]
    low = y == 2
    zero = nt(jnp.where(low, s2[...], s3[...]), f_ref[:, :size])
    both = jnp.concatenate([jnp.where(low, m1[...], m2[...]), s2[...]], 0)
    both = nt(both, f_ref[:, size:])
    out_ref[:m] = jnp.where(y >= 2, zero + both[:m], 0.0)
    out_ref[m:] = jnp.where(low, t1[...], jnp.where(y == 3, both[m:], 0.0))


def second_factor(place, s2, s3, m1, m2, t1, factor):
    m, bs = t1.shape
    args = (s2, s3, m1, m2, t1)
    return pl.pallas_call(
        second_factor_kernel,
        grid=(1,),
        in_specs=[SMEM]
        + [pl.BlockSpec(a.shape, lambda i: (0, 0)) for a in args]
        + [pl.BlockSpec((bs, 2 * SIDE * bs), lambda i: (0, 0))],
        out_specs=pl.BlockSpec((2 * m, bs), lambda i: (0, 0)),
        out_shape=jax.ShapeDtypeStruct((2 * m, bs), F32),
        compiler_params=PARAMS,
    )(place, *args, factor)


def interleave(full, mine, other, place):
    m = mine.shape[1]
    c, z = place[1], place[2]
    for k in range(ZS):
        at = 2 * jnp.bitwise_xor(z, k)
        full[pl.ds(pl.multiple_of((at + c) * m, m), m), :] = mine[k]
        full[pl.ds(pl.multiple_of((at + 1 - c) * m, m), m), :] = other[k]


def second_inverse_kernel(place, *refs):
    ts, qs, (st, mine, other, out_ref, t, q, full) = refs[:SIDE], refs[SIDE : 2 * SIDE], refs[2 * SIDE :]
    x, y = place[0], place[3]
    m, bs = ts[0].shape
    for k in range(SIDE):
        t[:, spot(k, x, bs)] = ts[k][...]
        q[:, spot(k, x, bs)] = qs[k][...]
    interleave(full, mine, other, place)
    total = mul3(split(t[...]), split(st[...]), NN)
    below = mul3(split(q[...]), split(full[...]), NN)
    total = total + jnp.where(y == 3, below, 0.0)
    half = m // 2
    out_ref[:half] = jnp.where(y >= 2, -total[:half], 0.0)
    out_ref[half:] = jnp.where(y == 3, -total[half:], 0.0)


def second_inverse(place, ts, qs, st, mine, other):
    m, bs = ts[0].shape
    size = SIDE * bs
    fixed = lambda a: pl.BlockSpec(a.shape, lambda i, p: (0,) * a.ndim)
    return pl.pallas_call(
        second_inverse_kernel,
        grid_spec=pltpu.PrefetchScalarGridSpec(
            num_scalar_prefetch=1,
            grid=(1,),
            in_specs=[fixed(a) for a in (*ts, *qs)]
            + [pl.BlockSpec((size, bs), lambda i, p: (0, p[0])), fixed(mine), fixed(other)],
            out_specs=pl.BlockSpec((m, bs), lambda i, p: (0, 0)),
            scratch_shapes=[pltpu.VMEM((m, size), F32)] * 2 + [pltpu.VMEM((size, bs), F32)],
        ),
        out_shape=jax.ShapeDtypeStruct((m, bs), F32),
        compiler_params=PARAMS,
    )(place, *ts, *qs, st, mine, other)


def panel_kernel(beta, train_ref, cand_ref, scale_ref, hi_ref, lo_ref):
    rows = train_ref[...]
    wide = rows.astype(F32)
    square = jnp.sum(wide * wide, axis=1, keepdims=True)
    row = jnp.broadcast_to(beta * lax.rsqrt(square + EPS), (rows.shape[0], 128)).T[:1]
    hi, lo = split(jnp.exp(mul(cand_ref[...], rows, NT) * row * scale_ref[...]))
    hi_ref[0] = hi
    lo_ref[0] = lo


def make_panel(train, cand, cand_scale, size):
    total, e = train.shape
    n = cand.shape[0]
    rows = size // 2
    spec = pl.BlockSpec((1, n, rows), lambda i: (i // 2, 0, i % 2))
    shape = jax.ShapeDtypeStruct((total // size, n, size), BF16)
    return pl.pallas_call(
        functools.partial(panel_kernel, 0.5 * math.sqrt(e)),
        grid=(total // rows,),
        in_specs=[
            pl.BlockSpec((rows, e), lambda i: (i, 0)),
            pl.BlockSpec((n, e), lambda i: (0, 0)),
            pl.BlockSpec((n, 1), lambda i: (0, 0)),
        ],
        out_specs=[spec, spec],
        out_shape=[shape, shape],
        cost_estimate=pl.CostEstimate(flops=4 * total * n * e, bytes_accessed=6 * total * n, transcendentals=total * n),
        compiler_params=PARAMS,
    )(train, cand, cand_scale)


def apply_kernel(last, sup, place, *refs):
    if last:
        m2, win, h0, l0, h1, l1, targets, out, mean, full, mh, ml = refs
    else:
        st, mine, other, h0, l0, h1, l1, out, full, mh, ml = refs
    size = full.shape[0]

    @pl.when(pl.program_id(0) == 0)
    def _():
        if last:
            m = size // (2 * ZS)
            for g in range(2 * ZS):
                full[g * m : (g + 1) * m] = m2[g, :m]
            mh[:size], ml[:size] = split(full[...])
            for g in range(2 * ZS):
                full[g * m : (g + 1) * m] = m2[g, m:]
        else:
            mh[:size], ml[:size] = split(st[...])
            interleave(full, mine, other, place)
        mh[size:], ml[size:] = split(full[...])

    w = mul3((h0[0], l0[0]), (mh[:size], ml[:size]), NN)
    w = w + mul3((h1[0], l1[0]), (mh[size:], ml[size:]), NN)
    if last:
        w = (w + win[...]).T
        out[...] = w
        mean[...] = jnp.sum(w * targets[...], axis=0, keepdims=True)
    else:
        out[...] = w


def apply(sup, place, arrays, panel, bs, targets=None):
    _, n, size = panel[0].shape
    last = targets is not None
    tile = n // 2
    fixed = lambda shape: pl.BlockSpec(shape, lambda i, s, p: (0,) * len(shape))
    args = [*arrays, *panel, *panel]
    specs = [fixed(a.shape) for a in arrays]
    across = pl.BlockSpec((tile, bs), lambda i, s, p: (i, 0))
    if last:
        specs[1] = across
    else:
        specs[0] = pl.BlockSpec((size, bs), lambda i, s, p: (0, p[0]))
    specs += [pl.BlockSpec((1, tile, size), lambda i, s, p: (s[0], i, 0))] * 2
    specs += [pl.BlockSpec((1, tile, size), lambda i, s, p: (s[1], i, 0))] * 2
    shapes, outs = [jax.ShapeDtypeStruct((n, bs), F32)], [across]
    if last:
        args.append(targets)
        specs.append(fixed(targets.shape))
        shapes = [jax.ShapeDtypeStruct((bs, n), F32), jax.ShapeDtypeStruct((1, n), F32)]
        outs = [pl.BlockSpec((bs, tile), lambda i, s, p: (0, i)), pl.BlockSpec((1, tile), lambda i, s, p: (0, i))]
    return pl.pallas_call(
        functools.partial(apply_kernel, last),
        grid_spec=pltpu.PrefetchScalarGridSpec(
            num_scalar_prefetch=2,
            grid=(n // tile,),
            in_specs=specs,
            out_specs=outs,
            scratch_shapes=[pltpu.VMEM((size, bs), F32)] + [pltpu.VMEM((2 * size, bs), BF16)] * 2,
        ),
        out_shape=shapes,
        cost_estimate=pl.CostEstimate(flops=24 * n * bs * size, bytes_accessed=8 * n * size, transcendentals=0),
        compiler_params=PARAMS,
    )(sup, place, *args)


def join_z(mine, bit):
    return jnp.concatenate([mine, send(mine, lambda y, x, z, c: (y, x, z ^ bit, c))], 0)


def shards(train_emb, cand_emb, factor, diag_inverse, targets):
    bs = diag_inverse.shape[1]
    n = cand_emb.shape[0]
    size = SIDE * bs
    p, z, c = (lax.axis_index(axis) for axis in AXES)
    y, x, group = p // SIDE, p % SIDE, 2 * z + c
    place = jnp.stack([x, c, z, y]).astype(jnp.int32)

    train = lax.all_gather(train_emb, AXES, axis=0, tiled=True)

    square = lax.dynamic_slice(factor, (0, y * size), (bs, size))
    pair0 = jnp.concatenate([diag_inverse, square[:, :bs]], 0)
    pair1 = jnp.concatenate([square[:, bs : 2 * bs], square[:, 2 * bs : 3 * bs]], 0)
    pair = jnp.where(c == 0, pair0, pair1)
    near = jnp.stack(
        [send(pair, lambda y, x, z, c: (y, (x + k) % SIDE, z, c) if c == 0 or x >= 2 else None) for k in (1, 2, 3)]
    )
    st = diagonal(place, diag_inverse, square, near, swap_core(near))

    m = size // (2 * ZS)
    sl = lax.dynamic_slice(st, (group * m, 0), (m, size))
    t1 = first_factor(place, hop(sl, 1), factor)
    t1, s2, s3 = lax.optimization_barrier((t1, hop(sl, 2), hop(sl, 3)))
    m1, m1_own = first_inverse(place, x_ring(t1), st)
    slices, up1, up2 = lax.optimization_barrier((join_z(m1_own[None], 1), hop(m1, 1), hop(m1, 2)))
    t2 = second_factor(place, s2, s3, up1, up2, t1, factor)
    slices, t2, *ts = lax.optimization_barrier((join_z(slices, 2), *x_ring(t2)))
    slices, *qs = lax.optimization_barrier((join_z(slices, 4), *[hop(t2, 1, k) for k in range(SIDE)]))
    m1_full = (slices, swap_core(slices))
    m2 = second_inverse(place, [t2, *ts], qs, st, *m1_full)
    m2_full = lax.all_gather(m2, ("z", "c"), axis=0)

    train, _ = lax.optimization_barrier((train, m2))
    cand_f = cand_emb.astype(F32)
    cand_scale = lax.rsqrt(jnp.sum(cand_f * cand_f, axis=1, keepdims=True) + EPS)
    panel = make_panel(train, cand_emb, cand_scale, size)
    sup = jnp.stack([y, jnp.maximum(y - 1, 0)]).astype(jnp.int32)
    (w,) = apply(sup, place, (st, *m1_full), panel, bs)
    w, mean = apply(jnp.arange(2, dtype=jnp.int32), place, (m2_full, w), panel, bs, targets.reshape(bs, 1))
    parts = lax.all_to_all(jnp.broadcast_to(mean, (CHAIN, n)), "chain", 0, 0, tiled=True)
    return w, jnp.sum(parts, axis=0)


def solution(mesh):
    fine = Mesh(mesh.devices.reshape(CHAIN, ZS, 2), AXES)
    group = ("z", "c")
    in_specs = (
        P(AXES, None),
        P(group, None),
        P("chain", None),
        P("chain", None),
        P("chain"),
    )
    out_specs = (P("chain", group), P(group))
    return jax.shard_map(shards, mesh=fine, in_specs=in_specs, out_specs=out_specs, check_vma=False)
```

```python
import functools
import math

import jax
import jax.numpy as jnp
from jax import lax
from jax.experimental import pallas as pl
from jax.experimental.pallas import tpu as pltpu
from jax.sharding import Mesh
from jax.sharding import PartitionSpec as P

EPS = 1e-06
BF16 = jnp.bfloat16
F32 = jnp.float32
AXES = ("chain", "z", "c")
SIDE = 4
ZS = 8
CHAIN = SIDE * SIDE
VMEM = pl.BlockSpec(memory_space=pltpu.VMEM)
SMEM = pl.BlockSpec(memory_space=pltpu.SMEM)
PARAMS = pltpu.CompilerParams(vmem_limit_bytes=56 * 1024 * 1024)


def moves(target):
    pairs = []
    for y in range(SIDE):
        for x in range(SIDE):
            for z in range(ZS):
                for c in range(2):
                    to = target(y, x, z, c)
                    if to is not None:
                        ty, tx, tz, tc = to
                        source = ((y * SIDE + x) * ZS + z) * 2 + c
                        dest = ((ty * SIDE + tx) * ZS + tz) * 2 + tc
                        pairs.append((source, dest))
    return pairs


def send(value, target):
    return lax.ppermute(value, AXES, moves(target))


def swap_core(value):
    return send(value, lambda y, x, z, c: (y, x, z, 1 - c))


def x_ring(value):
    return [value] + [send(value, lambda y, x, z, c: (y, (x + k) % SIDE, z, c)) for k in (1, 2, 3)]


def hop(value, dy, dx=0):
    return send(value, lambda y, x, z, c: (y + dy, (x + dx) % SIDE, z, c) if y + dy < SIDE else None)


def split(a):
    hi = a.astype(BF16)
    return hi, (a - hi.astype(F32)).astype(BF16)


def mul(a, b, dims):
    return lax.dot_general(a, b, (dims, ((), ())), preferred_element_type=F32)


NT = ((1,), (1,))
NN = ((1,), (0,))


def mul3(a, b, dims):
    (ah, al), (bh, bl) = a, b
    return mul(ah, bh, dims) + (mul(ah, bl, dims) + mul(al, bh, dims))


def nt(a, b):
    return mul3(split(a), split(b), NT)


def spot(k, x, bs):
    return pl.ds(pl.multiple_of(lax.rem(x - k + SIDE, SIDE) * bs, bs), bs)


def diagonal_kernel(place, d_ref, f_ref, near, far, out_ref, d, f):
    bs = d_ref.shape[0]
    x, c = place[0], place[1]
    own = (d_ref[...], f_ref[:, :bs], f_ref[:, bs : 2 * bs], f_ref[:, 2 * bs : 3 * bs])
    d[x] = own[0]
    for j in range(3):
        f[x, j] = own[1 + j]
    for k in (1, 2, 3):
        at = lax.rem(x - k + SIDE, SIDE)

        @pl.when(c == 0)
        def _():
            d[at], f[at, 0] = near[k - 1, :bs], near[k - 1, bs:]
            f[at, 1], f[at, 2] = far[k - 1, :bs], far[k - 1, bs:]

        @pl.when(c == 1)
        def _():
            d[at], f[at, 0] = far[k - 1, :bs], far[k - 1, bs:]
            f[at, 1], f[at, 2] = near[k - 1, :bs], near[k - 1, bs:]

    columns = []
    for i in range(SIDE):
        above = []
        for k in range(i):
            part = nt(columns[k], f[i, k])
            for j in range(k + 1):
                piece = part[j * bs : (j + 1) * bs]
                if j < len(above):
                    above[j] = above[j] + piece
                else:
                    above.append(piece)
        column = d[i].T
        if above:
            column = jnp.concatenate([-nt(jnp.concatenate(above, 0), d[i]), column], 0)
        columns.append(column)
        out_ref[: (i + 1) * bs, i * bs : (i + 1) * bs] = column
        if i < SIDE - 1:
            out_ref[(i + 1) * bs :, i * bs : (i + 1) * bs] = jnp.zeros(((SIDE - 1 - i) * bs, bs), F32)


def diagonal(place, d, factor, near, far):
    bs = d.shape[0]
    size = SIDE * bs
    fixed = lambda shape: pl.BlockSpec(shape, lambda i, p: (0,) * len(shape))
    return pl.pallas_call(
        diagonal_kernel,
        grid_spec=pltpu.PrefetchScalarGridSpec(
            num_scalar_prefetch=1,
            grid=(1,),
            in_specs=[
                fixed(d.shape),
                pl.BlockSpec((bs, size), lambda i, p: (0, p[3])),
                fixed(near.shape),
                fixed(far.shape),
            ],
            out_specs=fixed((size, size)),
            scratch_shapes=[pltpu.VMEM((SIDE, bs, bs), F32), pltpu.VMEM((SIDE, 3, bs, bs), F32)],
        ),
        out_shape=jax.ShapeDtypeStruct((size, size), F32),
        compiler_params=PARAMS,
    )(place, d, factor, near, far)


def first_factor_kernel(place, s_ref, f_ref, out_ref):
    out_ref[...] = nt(s_ref[...], f_ref[...])


def first_factor(place, s, factor):
    m, size = s.shape
    bs = factor.shape[0]
    return pl.pallas_call(
        first_factor_kernel,
        grid_spec=pltpu.PrefetchScalarGridSpec(
            num_scalar_prefetch=1,
            grid=(1,),
            in_specs=[
                pl.BlockSpec((m, size), lambda i, p: (0, 0)),
                pl.BlockSpec((bs, size), lambda i, p: (0, jnp.maximum(p[3] - 1, 0))),
            ],
            out_specs=pl.BlockSpec((m, bs), lambda i, p: (0, 0)),
        ),
        out_shape=jax.ShapeDtypeStruct((m, bs), F32),
        compiler_params=PARAMS,
    )(place, s, factor)


def first_inverse_kernel(place, t0, t1, t2, t3, st, out_ref, own_ref, t):
    x = place[0]
    bs = t0.shape[1]
    for k, ref in enumerate((t0, t1, t2, t3)):
        t[:, spot(k, x, bs)] = ref[...]
    th, tl = split(t[...])
    for i in range(SIDE):
        rows, columns = (i + 1) * bs, slice(i * bs, (i + 1) * bs)
        out_ref[:, columns] = -mul3((th[:, :rows], tl[:, :rows]), split(st[:rows, columns]), NN)
    own_ref[...] = out_ref[:, spot(0, x, bs)]


def first_inverse(place, ts, st):
    m, bs = ts[0].shape
    size = SIDE * bs
    return pl.pallas_call(
        first_inverse_kernel,
        in_specs=[SMEM] + [VMEM] * (SIDE + 1),
        out_specs=[VMEM, VMEM],
        out_shape=[jax.ShapeDtypeStruct((m, size), F32), jax.ShapeDtypeStruct((m, bs), F32)],
        scratch_shapes=[pltpu.VMEM((m, size), F32)],
        compiler_params=PARAMS,
    )(place, *ts, st)


def second_factor_kernel(place, s2, s3, m1, m2, t1, f_ref, out_ref):
    m, size = s2.shape
    y = place[3]
    low = y == 2
    zero = nt(jnp.where(low, s2[...], s3[...]), f_ref[:, :size])
    both = jnp.concatenate([jnp.where(low, m1[...], m2[...]), s2[...]], 0)
    both = nt(both, f_ref[:, size:])
    out_ref[:m] = jnp.where(y >= 2, zero + both[:m], 0.0)
    out_ref[m:] = jnp.where(low, t1[...], jnp.where(y == 3, both[m:], 0.0))


def second_factor(place, s2, s3, m1, m2, t1, factor):
    m, bs = t1.shape
    args = (s2, s3, m1, m2, t1)
    return pl.pallas_call(
        second_factor_kernel,
        grid=(1,),
        in_specs=[SMEM]
        + [pl.BlockSpec(a.shape, lambda i: (0, 0)) for a in args]
        + [pl.BlockSpec((bs, 2 * SIDE * bs), lambda i: (0, 0))],
        out_specs=pl.BlockSpec((2 * m, bs), lambda i: (0, 0)),
        out_shape=jax.ShapeDtypeStruct((2 * m, bs), F32),
        compiler_params=PARAMS,
    )(place, *args, factor)


def interleave(full, mine, other, place):
    m = mine.shape[1]
    c, z = place[1], place[2]
    for k in range(ZS):
        at = 2 * jnp.bitwise_xor(z, k)
        full[pl.ds(pl.multiple_of((at + c) * m, m), m), :] = mine[k]
        full[pl.ds(pl.multiple_of((at + 1 - c) * m, m), m), :] = other[k]


def second_inverse_kernel(place, *refs):
    ts, qs, (st, mine, other, out_ref, t, q, full) = refs[:SIDE], refs[SIDE : 2 * SIDE], refs[2 * SIDE :]
    x, y = place[0], place[3]
    m, bs = ts[0].shape
    for k in range(SIDE):
        t[:, spot(k, x, bs)] = ts[k][...]
        q[:, spot(k, x, bs)] = qs[k][...]
    interleave(full, mine, other, place)
    total = mul3(split(t[...]), split(st[...]), NN)
    below = mul3(split(q[...]), split(full[...]), NN)
    total = total + jnp.where(y == 3, below, 0.0)
    half = m // 2
    out_ref[:half] = jnp.where(y >= 2, -total[:half], 0.0)
    out_ref[half:] = jnp.where(y == 3, -total[half:], 0.0)


def second_inverse(place, ts, qs, st, mine, other):
    m, bs = ts[0].shape
    size = SIDE * bs
    fixed = lambda a: pl.BlockSpec(a.shape, lambda i, p: (0,) * a.ndim)
    return pl.pallas_call(
        second_inverse_kernel,
        grid_spec=pltpu.PrefetchScalarGridSpec(
            num_scalar_prefetch=1,
            grid=(1,),
            in_specs=[fixed(a) for a in (*ts, *qs)]
            + [pl.BlockSpec((size, bs), lambda i, p: (0, p[0])), fixed(mine), fixed(other)],
            out_specs=pl.BlockSpec((m, bs), lambda i, p: (0, 0)),
            scratch_shapes=[pltpu.VMEM((m, size), F32)] * 2 + [pltpu.VMEM((size, bs), F32)],
        ),
        out_shape=jax.ShapeDtypeStruct((m, bs), F32),
        compiler_params=PARAMS,
    )(place, *ts, *qs, st, mine, other)


def panel_kernel(beta, train_ref, cand_ref, scale_ref, hi_ref, lo_ref):
    rows = train_ref[...]
    wide = rows.astype(F32)
    square = jnp.sum(wide * wide, axis=1, keepdims=True)
    row = jnp.broadcast_to(beta * lax.rsqrt(square + EPS), (rows.shape[0], 128)).T[:1]
    hi, lo = split(jnp.exp(mul(cand_ref[...], rows, NT) * row * scale_ref[...]))
    hi_ref[0] = hi
    lo_ref[0] = lo


def make_panel(train, cand, cand_scale, size):
    total, e = train.shape
    n = cand.shape[0]
    rows = size // 2
    spec = pl.BlockSpec((1, n, rows), lambda i: (i // 2, 0, i % 2))
    shape = jax.ShapeDtypeStruct((total // size, n, size), BF16)
    return pl.pallas_call(
        functools.partial(panel_kernel, 0.5 * math.sqrt(e)),
        grid=(total // rows,),
        in_specs=[
            pl.BlockSpec((rows, e), lambda i: (i, 0)),
            pl.BlockSpec((n, e), lambda i: (0, 0)),
            pl.BlockSpec((n, 1), lambda i: (0, 0)),
        ],
        out_specs=[spec, spec],
        out_shape=[shape, shape],
        cost_estimate=pl.CostEstimate(flops=4 * total * n * e, bytes_accessed=6 * total * n, transcendentals=total * n),
        compiler_params=PARAMS,
    )(train, cand, cand_scale)


def apply_kernel(last, sup, place, *refs):
    if last:
        m2, win, h0, l0, h1, l1, targets, out, mean, full, mh, ml = refs
    else:
        st, mine, other, h0, l0, h1, l1, out, full, mh, ml = refs
    size = full.shape[0]

    @pl.when(pl.program_id(0) == 0)
    def _():
        if last:
            m = size // (2 * ZS)
            for g in range(2 * ZS):
                full[g * m : (g + 1) * m] = m2[g, :m]
            mh[:size], ml[:size] = split(full[...])
            for g in range(2 * ZS):
                full[g * m : (g + 1) * m] = m2[g, m:]
        else:
            mh[:size], ml[:size] = split(st[...])
            interleave(full, mine, other, place)
        mh[size:], ml[size:] = split(full[...])

    w = mul3((h0[0], l0[0]), (mh[:size], ml[:size]), NN)
    w = w + mul3((h1[0], l1[0]), (mh[size:], ml[size:]), NN)
    if last:
        w = (w + win[...]).T
        out[...] = w
        mean[...] = jnp.sum(w * targets[...], axis=0, keepdims=True)
    else:
        out[...] = w


def apply(sup, place, arrays, panel, bs, targets=None):
    _, n, size = panel[0].shape
    last = targets is not None
    tile = n // 2
    fixed = lambda shape: pl.BlockSpec(shape, lambda i, s, p: (0,) * len(shape))
    args = [*arrays, *panel, *panel]
    specs = [fixed(a.shape) for a in arrays]
    across = pl.BlockSpec((tile, bs), lambda i, s, p: (i, 0))
    if last:
        specs[1] = across
    else:
        specs[0] = pl.BlockSpec((size, bs), lambda i, s, p: (0, p[0]))
    specs += [pl.BlockSpec((1, tile, size), lambda i, s, p: (s[0], i, 0))] * 2
    specs += [pl.BlockSpec((1, tile, size), lambda i, s, p: (s[1], i, 0))] * 2
    shapes, outs = [jax.ShapeDtypeStruct((n, bs), F32)], [across]
    if last:
        args.append(targets)
        specs.append(fixed(targets.shape))
        shapes = [jax.ShapeDtypeStruct((bs, n), F32), jax.ShapeDtypeStruct((1, n), F32)]
        outs = [pl.BlockSpec((bs, tile), lambda i, s, p: (0, i)), pl.BlockSpec((1, tile), lambda i, s, p: (0, i))]
    return pl.pallas_call(
        functools.partial(apply_kernel, last),
        grid_spec=pltpu.PrefetchScalarGridSpec(
            num_scalar_prefetch=2,
            grid=(n // tile,),
            in_specs=specs,
            out_specs=outs,
            scratch_shapes=[pltpu.VMEM((size, bs), F32)] + [pltpu.VMEM((2 * size, bs), BF16)] * 2,
        ),
        out_shape=shapes,
        cost_estimate=pl.CostEstimate(flops=24 * n * bs * size, bytes_accessed=8 * n * size, transcendentals=0),
        compiler_params=PARAMS,
    )(sup, place, *args)


def join_z(mine, bit):
    return jnp.concatenate([mine, send(mine, lambda y, x, z, c: (y, x, z ^ bit, c))], 0)


def shards(train_emb, cand_emb, factor, diag_inverse, targets):
    bs = diag_inverse.shape[1]
    n = cand_emb.shape[0]
    size = SIDE * bs
    p, z, c = (lax.axis_index(axis) for axis in AXES)
    y, x, group = p // SIDE, p % SIDE, 2 * z + c
    place = jnp.stack([x, c, z, y]).astype(jnp.int32)

    train = lax.all_gather(train_emb, AXES, axis=0, tiled=True)

    square = lax.dynamic_slice(factor, (0, y * size), (bs, size))
    pair0 = jnp.concatenate([diag_inverse, square[:, :bs]], 0)
    pair1 = jnp.concatenate([square[:, bs : 2 * bs], square[:, 2 * bs : 3 * bs]], 0)
    pair = jnp.where(c == 0, pair0, pair1)
    near = jnp.stack(
        [send(pair, lambda y, x, z, c: (y, (x + k) % SIDE, z, c) if c == 0 or x >= 2 else None) for k in (1, 2, 3)]
    )
    st = diagonal(place, diag_inverse, factor, near, swap_core(near))

    m = size // (2 * ZS)
    sl = lax.dynamic_slice(st, (group * m, 0), (m, size))
    t1 = first_factor(place, hop(sl, 1), factor)
    t1, s2, s3 = lax.optimization_barrier((t1, hop(sl, 2), hop(sl, 3)))
    m1, m1_own = first_inverse(place, x_ring(t1), st)
    slices, up1, up2 = lax.optimization_barrier((join_z(m1_own[None], 1), hop(m1, 1), hop(m1, 2)))
    t2 = second_factor(place, s2, s3, up1, up2, t1, factor)
    slices, t2, *ts = lax.optimization_barrier((join_z(slices, 2), *x_ring(t2)))
    slices, *qs = lax.optimization_barrier((join_z(slices, 4), *[hop(t2, 1, k) for k in range(SIDE)]))
    m1_full = (slices, swap_core(slices))
    m2 = second_inverse(place, [t2, *ts], qs, st, *m1_full)
    m2_full = lax.all_gather(m2, ("z", "c"), axis=0)

    train, _ = lax.optimization_barrier((train, m2))
    cand_f = cand_emb.astype(F32)
    cand_scale = lax.rsqrt(jnp.sum(cand_f * cand_f, axis=1, keepdims=True) + EPS)
    panel = make_panel(train, cand_emb, cand_scale, size)
    sup = jnp.stack([y, jnp.maximum(y - 1, 0)]).astype(jnp.int32)
    (w,) = apply(sup, place, (st, *m1_full), panel, bs)
    w, mean = apply(jnp.arange(2, dtype=jnp.int32), place, (m2_full, w), panel, bs, targets.reshape(bs, 1))
    parts = lax.all_to_all(jnp.broadcast_to(mean, (CHAIN, n)), "chain", 0, 0, tiled=True)
    return w, jnp.sum(parts, axis=0)


def solution(mesh):
    fine = Mesh(mesh.devices.reshape(CHAIN, ZS, 2), AXES)
    group = ("z", "c")
    in_specs = (
        P(AXES, None),
        P(group, None),
        P("chain", None),
        P("chain", None),
        P("chain"),
    )
    out_specs = (P("chain", group), P(group))
    return jax.shard_map(shards, mesh=fine, in_specs=in_specs, out_specs=out_specs, check_vma=False)
```
